256 devices in a mesh: snap: 8 (over z_lo, y), chan: 32 (over x, z_hi, core).
Axes of the slice: x: 4, y: 4, z: 8 (z_hi: 4, z_lo: 2; z = z_hi * 2 + z_lo), core: 2. Of those that a mesh axis runs over, the one named last changes fastest.
Arguments:
- snap_tiles: bfloat16 [64, 192, 64, 128], P('snap', 'chan'), may hold values from -6 to 6
- beam_gain: float32 [64, 64, 128], P('snap'), may hold values from 0.1 to 1
- kernel: bfloat16 [64, 128, 128, 256], P(None, 'snap'), may hold values from -0.5 to 0.5
- tile_map: int32 [64, 128], replicated, may hold values from 0 to 63
- pixel_lm: float32 [2, 32768], P(None, 'snap'), may hold values from -0.5 to 0.5
- mode_uv: int32 [2, 2048], replicated, may hold values from -32 to 31
Outputs:
- sky_cube: float32 [128, 192, 256], P('snap', 'chan')
- delay_spec: float32 [2, 192, 2048], P(None, None, ('snap', 'chan'))
The draws below stay inside these ranges and needn't reach their ends.
Inputs may be any that keep to these rules, and one draw needn't show every extreme that they name: `tile_map`: tile indices.
All inputs are finite; a program needn't handle non-finite values.
Results may differ from the reference program's by a relative error of at most 0.0047.
Values may be sent and summed in bfloat16 or wider, within the bound.
A program may use at most 192 MiB of HBM per device.

```python
import math
import jax
import jax.numpy as jnp
from jax import lax

SNAPS = 64
CHANS = 192
TILES = 64
TILE_PIX = 128
BLOCK_PIX = 256
PIXELS = 32768
BLOCKS = 128
MODES = 2048
UV_MAX = 32


def place_ends(array, rng, least, top_value):
    place = [jax.random.randint(jax.random.fold_in(rng, axis), (), 0, length) for axis, length in enumerate(array.shape)]
    longest = array.shape.index(max(array.shape))
    next_to = place[:longest] + [(place[longest] + 1) % array.shape[longest]] + place[longest + 1:]
    return array.at[tuple(place)].set(least).at[tuple(next_to)].set(top_value)


def block_levels(own_key, shape, pieces, smallest, top_value):
    gain = 1.0
    for dim, parts in pieces:
        heights = jax.random.uniform(jax.random.fold_in(jax.random.fold_in(own_key, 6), dim), (parts,), jnp.float32, smallest / len(pieces), top_value / len(pieces))
        gain = gain * jnp.repeat(jnp.exp(heights), shape[dim] // parts).reshape((-1,) + (1,) * (len(shape) - 1 - dim))
    return gain


def scatter_about(own_key, shape, scale, most, cuts=(), kind=jnp.bfloat16):
    array = jax.random.normal(own_key, shape, jnp.float32) * scale
    if len(cuts) > 0:
        array = block_levels(own_key, shape, cuts, -0.22, 0.18) * array
    return jnp.clip(array, min=-most, max=most).astype(kind)


def setup_inputs(seed: int = 0) -> dict:
    key_of = jax.random.split(jax.random.key(seed), 7)
    return {
        "snap_tiles": scatter_about(key_of[0], (SNAPS, CHANS, TILES, TILE_PIX), 1.0, 6.0, ((0, 8), (1, 32))),
        "beam_gain": jnp.clip(jnp.exp(math.log(1.0) - 2.3025851 * jax.random.uniform(key_of[1], (SNAPS, TILES, TILE_PIX), jnp.float32) ** block_levels(key_of[1], (SNAPS, TILES, TILE_PIX), ((0, 8),), -0.2, 0.2)), 0.1, 1.0),
        "kernel": scatter_about(key_of[2], (SNAPS, BLOCKS, TILE_PIX, BLOCK_PIX), TILE_PIX ** -0.5, 0.5, ((1, 8),)),
        "tile_map": place_ends(jax.random.randint(key_of[3], (SNAPS, BLOCKS), 0, TILES), jax.random.fold_in(key_of[3], 1), 0, TILES - 1).astype(jnp.int32),
        "pixel_lm": jnp.clip(jax.random.uniform(key_of[4], (2, PIXELS), jnp.float32, -0.5, 0.5) * block_levels(key_of[4], (2, PIXELS), ((1, 8),), -0.4, 0.0), -0.5, 0.5),
        "mode_uv": place_ends(jax.random.randint(key_of[5], (2, MODES), 0 - UV_MAX, UV_MAX), jax.random.fold_in(key_of[5], 1), 0 - UV_MAX, UV_MAX - 1).astype(jnp.int32),
    }


def hamming(length):
    channel_index = jnp.arange(length, dtype=jnp.float32)
    return 0.54 - 0.46 * jnp.cos(channel_index * (2.0 * math.pi / (length - 1)))

def delay_transform(power_spectrum):
    length = power_spectrum.shape[1]
    channel_index = jnp.arange(length, dtype=jnp.int32)
    residues = channel_index[:, None] * channel_index[None, :] % length
    phases = residues.astype(jnp.float32) * (2.0 * math.pi / length)
    cosine = jnp.cos(phases)
    sine_part = jnp.sin(phases)
    window_gain = hamming(length)[:, None]
    real_component = power_spectrum[0] * window_gain
    imag_part = power_spectrum[1] * window_gain
    highest = lax.Precision.HIGHEST
    out_re = jnp.dot(cosine, real_component, precision=highest) + jnp.dot(sine_part, imag_part, precision=highest)
    out_im = jnp.dot(cosine, imag_part, precision=highest) - jnp.dot(sine_part, real_component, precision=highest)
    return jnp.stack([out_re, out_im]) / math.sqrt(length)

def phasor(positions, uv_grid):
    spatial = uv_grid.astype(jnp.float32)
    phase_table = (positions[0][:, None] * spatial[0][None, :] + positions[1][:, None] * spatial[1][None, :]) * (2.0 * math.pi)
    return jnp.concatenate([jnp.cos(phase_table), -jnp.sin(phase_table)], axis=1).astype(jnp.bfloat16)

def reference(snap_tiles, beam_gain, kernel, tile_map, pixel_lm, mode_uv):
    weighted = (snap_tiles.astype(jnp.float32) * beam_gain[:, None]).astype(jnp.bfloat16)

    def add_snapshot(running, inputs):
        single_snapshot_tiles, one_kernel, one_map = inputs
        gathered_rows = jnp.take(single_snapshot_tiles, one_map.astype(jnp.int32), axis=1)
        block_term = jnp.einsum('cbt,btp->bcp', gathered_rows.astype(jnp.float32), one_kernel.astype(jnp.float32))
        return (running + block_term, None)
    zero_cube = jnp.zeros((BLOCKS, CHANS, BLOCK_PIX), jnp.float32)
    sky_cube, _ = lax.scan(add_snapshot, zero_cube, (weighted, kernel, tile_map))
    cube_low = sky_cube.astype(jnp.bfloat16)
    lm_blocks = pixel_lm.reshape(2, BLOCKS, BLOCK_PIX).transpose(1, 0, 2)

    def add_block(running, inputs):
        block_cube, block_lm = inputs
        phasor_lookup = phasor(block_lm, mode_uv)
        return (running + jnp.dot(block_cube, phasor_lookup, preferred_element_type=jnp.float32), None)
    zero_modes = jnp.zeros((CHANS, 2 * MODES), jnp.float32)
    summed, _ = lax.scan(add_block, zero_modes, (cube_low, lm_blocks))
    uv_modes = (summed / math.sqrt(PIXELS)).reshape(CHANS, 2, MODES).transpose(1, 0, 2)
    delay_spec = delay_transform(uv_modes)
    return (sky_cube, delay_spec)
```

```python
import functools
import math

import jax
import jax.numpy as jnp
import numpy as np
from jax import lax
from jax.experimental import pallas as pl
from jax.experimental.pallas import tpu as pltpu
from jax.sharding import PartitionSpec as P

MESH = pl.DeviceIdType.MESH
X = 4
Z = 2
TILES = 64
TILE_PIX = 128
BLOCK_PIX = 256
OWN = 4
SN = 8
CH = 6
ROWS = X * 8
HALF = 64
F32 = jnp.float32
BF16 = jnp.bfloat16


def cosine_coefficients():
    fit = np.polynomial.chebyshev.Chebyshev.interpolate(
        lambda t: np.cos(2 * np.pi * np.sqrt(np.maximum(t, 0))), 5, domain=[0, 0.25]
    )
    return [float(c) for c in fit.convert(kind=np.polynomial.Polynomial).coef]


COS = cosine_coefficients()


def delay_matrices(groups, pixels):
    chans = groups * X * CH
    chan = np.arange(chans)
    window = 0.54 - 0.46 * np.cos(chan * (2 * math.pi / (chans - 1)))
    phase = (chan[:, None] * chan[None, :] % chans) * (2 * math.pi / chans)
    scale = window / math.sqrt(chans) / math.sqrt(pixels)
    out = np.zeros((2, chans, groups * ROWS), np.float32)
    for zc in range(groups):
        for xr in range(X):
            col = zc * ROWS + xr * 8
            first = (xr * groups + zc) * CH
            part = slice(first, first + CH)
            out[0, :, col : col + CH] = np.cos(phase[:, part]) * scale[part]
            out[1, :, col : col + CH] = np.sin(phase[:, part]) * scale[part]
    return out


def kernel_body(
    S, G, tiles, beam, kern, tmap, lm, uv, mats, sky, delay,
    kbuf, ph, send, recv, unp, acc, uvs, cubes, ubuf, g1, g2,
    k_sem, b_send, b_recv, d_send, d_recv, g1_send, g1_recv, g2_send, g2_recv,
):
    Y = S // Z
    D = S * X
    snap = lax.axis_index("snap")
    chan = lax.axis_index("chan")
    x, zc = chan // G, chan % G
    z, y = snap // Y, snap % Y
    me = snap * X + x

    def dev(to_snap, to_x, to_zc):
        return {"snap": to_snap, "chan": to_x * G + to_zc}

    def offsets(g):
        oz = g % 2
        return oz, (g // 2 + 2 * oz) % Y

    def source(g):
        oz, oy = offsets(g)
        return ((z + oz) % Z) * Y + (y + Y - oy) % Y

    def fetch(src):
        return pltpu.make_async_copy(
            kern.at[pl.ds(src * SN, SN), pl.ds(x * OWN, OWN)], kbuf.at[src], k_sem.at[src]
        )

    barrier = pltpu.get_barrier_semaphore()

    @pl.loop(1, D)
    def _(o):
        other = (me + o) % D
        pl.semaphore_signal(
            barrier, inc=1, device_id=dev(other // X, other % X, zc), device_id_type=MESH
        )

    @pl.loop(1, G)
    def _(o):
        pl.semaphore_signal(
            barrier, inc=1, device_id=dev(snap, x, (zc + o) % G), device_id_type=MESH
        )

    @pl.loop(0, S)
    def _(g):
        fetch(source(g)).start()

    rows = D * 16
    blocks = D * OWN
    r_row = lax.broadcasted_iota(jnp.int32, (rows, blocks), 0)
    r_col = lax.broadcasted_iota(jnp.int32, (rows, blocks), 1)
    spread = jnp.where(r_col == (r_row // 16) * OWN + r_row % OWN, 1.0, 0.0).astype(BF16)
    k_row = lax.broadcasted_iota(jnp.int32, (rows, 4 * TILES), 0)
    k_col = lax.broadcasted_iota(jnp.int32, (rows, 4 * TILES), 1)
    same = (k_row // 4) % 4 == k_col // TILES
    wanted = jnp.where(same, k_col % TILES, -1).astype(F32)
    own_map = tmap[pl.ds(pl.multiple_of(snap * SN, SN), SN), :].astype(F32)
    for q in range(2):
        wide = jnp.concatenate(
            [jnp.broadcast_to(own_map[q * 4 + j : q * 4 + j + 1], (TILES, blocks)) for j in range(4)],
            axis=0,
        ).astype(BF16)
        found = lax.dot_general(
            spread, wide, (((1,), (1,)), ((), ())), preferred_element_type=F32
        )
        onehot = jnp.where(found == wanted, 1.0, 0.0).astype(BF16)
        gain = beam[q * 4 : q * 4 + 4].reshape(4 * TILES, TILE_PIX)
        for c in range(0, CH, 2):
            pair = [
                (
                    tiles[q * 4 : q * 4 + 4, c + i].reshape(4 * TILES, TILE_PIX).astype(F32) * gain
                ).astype(BF16)
                for i in range(2)
            ]
            taken = jnp.dot(
                onehot, jnp.concatenate(pair, axis=1), preferred_element_type=F32
            ).astype(BF16)
            for i in range(2):
                send[:, q, c + i] = taken[:, i * TILE_PIX : (i + 1) * TILE_PIX].reshape(
                    D, 16, TILE_PIX
                )

    pl.semaphore_wait(barrier, D - 1 + G - 1)

    def tile_copy(o):
        oz, oy = offsets(o // X)
        to_snap = ((z + oz) % Z) * Y + (y + oy) % Y
        to_x = (x + o % X) % X
        to = to_snap * X + to_x
        return pltpu.make_async_remote_copy(
            src_ref=send.at[to],
            dst_ref=recv.at[snap, x],
            send_sem=b_send.at[to],
            recv_sem=b_recv.at[snap],
            device_id=dev(to_snap, to_x, zc),
            device_id_type=MESH,
        )

    @pl.loop(1, D)
    def _(o):
        tile_copy(o).start()

    recv[snap, x] = send[me]

    lane = lax.broadcasted_iota(jnp.int32, (1, 2 * HALF), 1)
    turn = jnp.where(lane < HALF, 0.0, 0.25).astype(F32)
    for s in range(S):
        at = pl.multiple_of((s * X + (x // 2) * 2) * HALF, 2 * HALF)
        seg = uv[:, pl.ds(at, 2 * HALF)].astype(F32)
        swapped = jnp.concatenate([seg[:, HALF:], seg[:, :HALF]], axis=1)
        keep = lane // HALF == x % 2
        uvs[s] = jnp.where(keep, seg, swapped)
    unp[...] = jnp.zeros_like(unp)
    acc[...] = jnp.zeros_like(acc)

    def phasor_rows(i):
        at = pl.multiple_of(i * 128, 128)
        left = jnp.broadcast_to(lm[0:1, pl.ds(at, 128)], (128, 128)).T
        right = jnp.broadcast_to(lm[1:2, pl.ds(at, 128)], (128, 128)).T
        for s in range(S):
            turns = left * uvs[s, 0:1] + right * uvs[s, 1:2] + turn
            rest = turns - jnp.round(turns)
            t = rest * rest
            value = jnp.full_like(t, COS[-1])
            for coefficient in COS[-2::-1]:
                value = value * t + coefficient
            ph[pl.ds(at, 128), s * 128 : (s + 1) * 128] = value.astype(BF16)

    parts = X * OWN * BLOCK_PIX // 128 // S

    @pl.loop(0, S)
    def _(g):
        @pl.loop(0, parts)
        def _(i):
            phasor_rows(g * parts + i)

        src = source(g)
        fetch(src).wait()

        @pl.when(g == 0)
        def _():
            part = recv.at[snap, pl.ds(0, X - 1)]
            pltpu.make_async_copy(part, part, b_recv.at[snap]).wait()

        @pl.when(g > 0)
        def _():
            pltpu.make_async_copy(recv.at[src], recv.at[src], b_recv.at[src]).wait()

        for xs in range(X):
            for q in range(2):
                unp[xs * 2 + q, 0 : CH * 16] = (
                    recv[src, xs, q].reshape(CH * 16, TILE_PIX).astype(F32)
                )
        for b in range(OWN):
            lhs = jnp.concatenate(
                [
                    jnp.concatenate(
                        [unp[xs * 2 + q, pl.ds(j * 4 + b, 8, stride=16)] for xs in range(X)], axis=0
                    ).astype(BF16)
                    for q in range(2)
                    for j in range(4)
                ],
                axis=1,
            )
            weights = kbuf[src, :, b].reshape(SN * TILE_PIX, BLOCK_PIX)
            acc[b] += jnp.dot(lhs, weights, preferred_element_type=F32)

    cubes[x] = acc[...].astype(BF16)

    def cube_copy(o):
        to = (x + o) % X
        return pltpu.make_async_remote_copy(
            src_ref=cubes.at[x],
            dst_ref=cubes.at[x],
            send_sem=d_send.at[o],
            recv_sem=d_recv.at[x],
            device_id=dev(snap, to, zc),
            device_id_type=MESH,
        )

    @pl.loop(1, X)
    def _(o):
        cube_copy(o).start()

    def transform(xs, first):
        for b in range(OWN):
            at = pl.multiple_of((xs * OWN + b) * BLOCK_PIX, BLOCK_PIX)
            part = jnp.dot(
                cubes[xs, b], ph[pl.ds(at, BLOCK_PIX), :], preferred_element_type=F32
            )
            total = part if b == 0 else total + part
        for s in range(S):
            piece = total[:, s * 128 : (s + 1) * 128]
            ubuf[s] = piece if first else ubuf[s] + piece

    transform(x, True)

    @pl.loop(1, X)
    def _(o):
        xs = (x + X - o) % X
        pltpu.make_async_copy(cubes.at[xs], cubes.at[xs], d_recv.at[xs]).wait()
        transform(xs, False)

    def sum_copy(o):
        to = (snap + o) % S
        return pltpu.make_async_remote_copy(
            src_ref=ubuf.at[to],
            dst_ref=g1.at[snap],
            send_sem=g1_send.at[o],
            recv_sem=g1_recv.at[0],
            device_id=dev(to, x, zc),
            device_id_type=MESH,
        )

    @pl.loop(1, S)
    def _(o):
        sum_copy(o).start()

    g1[snap] = ubuf[snap]

    for xs in range(X):
        for b in range(OWN):
            whole = cubes[xs, b].astype(F32)
            mine = whole[0:8]
            for k in range(1, X):
                mine = jnp.where(x == k, whole[k * 8 : k * 8 + 8], mine)
            sky[xs * OWN + b] = mine[:CH]

    pltpu.make_async_copy(g1.at[pl.ds(0, S - 1)], g1.at[pl.ds(0, S - 1)], g1_recv.at[0]).wait()
    g2[zc] = jnp.sum(g1[...], axis=0)

    def mode_copy(o):
        return pltpu.make_async_remote_copy(
            src_ref=g2.at[zc],
            dst_ref=g2.at[zc],
            send_sem=g2_send.at[o],
            recv_sem=g2_recv.at[0],
            device_id=dev(snap, x, (zc + o) % G),
            device_id_type=MESH,
        )

    @pl.loop(1, G)
    def _(o):
        mode_copy(o).start()

    pltpu.make_async_copy(g2.at[pl.ds(0, G - 1)], g2.at[pl.ds(0, G - 1)], g2_recv.at[0]).wait()

    modes = g2[...].reshape(G * ROWS, 2 * HALF)
    exact = lax.Precision.HIGHEST
    by_cos = jnp.dot(mats[0], modes, precision=exact, preferred_element_type=F32)
    by_sin = jnp.dot(mats[1], modes, precision=exact, preferred_element_type=F32)
    turned = pltpu.roll(by_sin, HALF, 1)
    spec = by_cos + jnp.where(lane < HALF, turned, -turned)
    each = HALF // G
    spec = pltpu.roll(spec, (2 * HALF - zc * each) % (2 * HALF), 1)
    delay[0] = spec[:, 0:each]
    delay[1] = spec[:, HALF : HALF + each]

    @pl.loop(1, D)
    def _(o):
        tile_copy(o).wait_send()

    @pl.loop(1, X)
    def _(o):
        cube_copy(o).wait_send()

    @pl.loop(1, S)
    def _(o):
        sum_copy(o).wait_send()

    @pl.loop(1, G)
    def _(o):
        mode_copy(o).wait_send()


def per_device(snap_tiles, beam_gain, kernel, tile_map, pixel_lm, mode_uv):
    S = lax.axis_size("snap")
    G = lax.axis_size("chan") // X
    pixels = pixel_lm.shape[1]
    mats = jnp.asarray(delay_matrices(G, pixels * S))
    chans = G * X * CH
    vmem = pl.BlockSpec(memory_space=pltpu.VMEM)
    dma = pltpu.SemaphoreType.DMA
    return pl.pallas_call(
        functools.partial(kernel_body, S, G),
        out_shape=(
            jax.ShapeDtypeStruct((X * OWN, CH, BLOCK_PIX), F32),
            jax.ShapeDtypeStruct((2, chans, HALF // G), F32),
        ),
        in_specs=[vmem, vmem, pl.BlockSpec(memory_space=pl.ANY), vmem, vmem, vmem, vmem],
        out_specs=(vmem, vmem),
        scratch_shapes=[
            pltpu.VMEM((S, SN, OWN, TILE_PIX, BLOCK_PIX), BF16),
            pltpu.VMEM((pixels, S * 2 * HALF), BF16),
            pltpu.VMEM((S * X, 2, CH, 16, TILE_PIX), BF16),
            pltpu.VMEM((S, X, 2, CH, 16, TILE_PIX), BF16),
            pltpu.VMEM((X * 2, 128, TILE_PIX), F32),
            pltpu.VMEM((OWN, ROWS, BLOCK_PIX), F32),
            pltpu.VMEM((S, 2, 2 * HALF), F32),
            pltpu.VMEM((X, OWN, ROWS, BLOCK_PIX), BF16),
            pltpu.VMEM((S, ROWS, 2 * HALF), F32),
            pltpu.VMEM((S, ROWS, 2 * HALF), F32),
            pltpu.VMEM((G, ROWS, 2 * HALF), F32),
            dma((S,)),
            dma((S * X,)),
            dma((S,)),
            dma((X,)),
            dma((X,)),
            dma((S,)),
            dma((1,)),
            dma((G,)),
            dma((1,)),
        ],
        compiler_params=pltpu.CompilerParams(
            collective_id=0, has_side_effects=True, vmem_limit_bytes=52 * 1024 * 1024
        ),
    )(snap_tiles, beam_gain, kernel, tile_map, pixel_lm, mode_uv, mats)


def solution(mesh):
    return jax.shard_map(
        per_device,
        mesh=mesh,
        in_specs=(
            P("snap", "chan", None, None),
            P("snap", None, None),
            P(None, "snap", None, None),
            P(),
            P(None, "snap"),
            P(),
        ),
        out_specs=(P("snap", "chan", None), P(None, None, ("snap", "chan"))),
        check_vma=False,
    )
```

```python
import functools
import math

import jax
import jax.numpy as jnp
import ml_dtypes
import numpy as np
from jax import lax
from jax.experimental import pallas as pl
from jax.experimental.pallas import tpu as pltpu
from jax.sharding import PartitionSpec as P

MESH = pl.DeviceIdType.MESH
X = 4
Z = 2
TILES = 64
TILE_PIX = 128
BLOCK_PIX = 256
OWN = 4
SN = 8
CH = 6
ROWS = X * 8
HALF = 64
SIN = 256
F32 = jnp.float32
BF16 = jnp.bfloat16


def cosine_coefficients():
    fit = np.polynomial.chebyshev.Chebyshev.interpolate(
        lambda t: np.cos(2 * np.pi * np.sqrt(np.maximum(t, 0))), 5, domain=[0, 0.25]
    )
    return [float(c) for c in fit.convert(kind=np.polynomial.Polynomial).coef]


COS = cosine_coefficients()


def delay_matrices(groups, pixels):
    chans = groups * X * CH
    chan = np.arange(chans)
    window = 0.54 - 0.46 * np.cos(chan * (2 * math.pi / (chans - 1)))
    phase = (chan[:, None] * chan[None, :] % chans) * (2 * math.pi / chans)
    scale = window / math.sqrt(chans) / math.sqrt(pixels)
    out = np.zeros((groups * ROWS, 2 * SIN), np.float32)
    for zc in range(groups):
        for xr in range(X):
            row = zc * ROWS + xr * 8
            first = (xr * groups + zc) * CH
            part = slice(first, first + CH)
            out[row : row + CH, :chans] = np.cos(phase[part]) * scale[part, None]
            out[row : row + CH, SIN : SIN + chans] = np.sin(phase[part]) * scale[part, None]
    high = out.astype(ml_dtypes.bfloat16)
    low = (out - high.astype(np.float32)).astype(ml_dtypes.bfloat16)
    return np.stack([high, low])


def kernel_body(
    S, G, tiles_hbm, beam_hbm, kern, tmap_hbm, lm_hbm, uv_hbm, mats_hbm, sky, delay,
    tiles, beam, tmap, lm, uv, mats, in_sem, kbuf, ph, send, recv, unp, acc, uvs, cubes, ubuf, g1, g2_out, g2,
    k_sem, b_send, b_recv, d_send, d_recv, g1_send, g1_recv, g2_send, g2_recv,
):
    Y = S // Z
    D = S * X
    snap = lax.axis_index("snap")
    chan = lax.axis_index("chan")
    x, zc = chan // G, chan % G
    z, y = snap // Y, snap % Y
    me = snap * X + x

    def dev(to_snap, to_x, to_zc):
        return {"snap": to_snap, "chan": to_x * G + to_zc}

    def offsets(g):
        oz = g % 2
        return oz, (g // 2 + 2 * oz) % Y

    def source(g):
        oz, oy = offsets(g)
        return ((z + oz) % Z) * Y + (y + Y - oy) % Y

    def fetch(src):
        return pltpu.make_async_copy(
            kern.at[pl.ds(src * SN, SN), pl.ds(x * OWN, OWN)], kbuf.at[src], k_sem.at[src]
        )

    inputs = [
        pltpu.make_async_copy(far, near, in_sem.at[i])
        for i, (far, near) in enumerate(
            [
                (tmap_hbm, tmap), (tiles_hbm, tiles), (beam_hbm, beam),
                (uv_hbm, uv), (lm_hbm, lm), (mats_hbm, mats),
            ]
        )
    ]
    for copy in inputs:
        copy.start()

    barrier = pltpu.get_barrier_semaphore()

    @pl.loop(1, D)
    def _(o):
        other = (me + o) % D
        pl.semaphore_signal(
            barrier, inc=1, device_id=dev(other // X, other % X, zc), device_id_type=MESH
        )

    @pl.loop(1, G)
    def _(o):
        pl.semaphore_signal(
            barrier, inc=1, device_id=dev(snap, x, (zc + o) % G), device_id_type=MESH
        )

    @pl.loop(0, S)
    def _(g):
        fetch(source(g)).start()

    rows = D * 16
    blocks = D * OWN
    r_row = lax.broadcasted_iota(jnp.int32, (rows, blocks), 0)
    r_col = lax.broadcasted_iota(jnp.int32, (rows, blocks), 1)
    spread = jnp.where(r_col == (r_row // 16) * OWN + r_row % OWN, 1.0, 0.0).astype(BF16)
    k_row = lax.broadcasted_iota(jnp.int32, (rows, 4 * TILES), 0)
    k_col = lax.broadcasted_iota(jnp.int32, (rows, 4 * TILES), 1)
    same = (k_row // 4) % 4 == k_col // TILES
    wanted = jnp.where(same, k_col % TILES, -1).astype(F32)
    inputs[0].wait()
    own_map = tmap[pl.ds(pl.multiple_of(snap * SN, SN), SN), :].astype(F32)
    for q in range(2):
        wide = jnp.concatenate(
            [jnp.broadcast_to(own_map[q * 4 + j : q * 4 + j + 1], (TILES, blocks)) for j in range(4)],
            axis=0,
        ).astype(BF16)
        found = lax.dot_general(
            spread, wide, (((1,), (1,)), ((), ())), preferred_element_type=F32
        )
        if q == 0:
            inputs[1].wait()
            inputs[2].wait()
        onehot = jnp.where(found == wanted, 1.0, 0.0).astype(BF16)
        gain = beam[q * 4 : q * 4 + 4].reshape(4 * TILES, TILE_PIX)
        for c in range(0, CH, 2):
            pair = [
                (
                    tiles[q * 4 : q * 4 + 4, c + i].reshape(4 * TILES, TILE_PIX).astype(F32) * gain
                ).astype(BF16)
                for i in range(2)
            ]
            taken = jnp.dot(
                onehot, jnp.concatenate(pair, axis=1), preferred_element_type=F32
            ).astype(BF16)
            for i in range(2):
                send[:, q, c + i] = taken[:, i * TILE_PIX : (i + 1) * TILE_PIX].reshape(
                    D, 16, TILE_PIX
                )

    pl.semaphore_wait(barrier, D - 1 + G - 1)

    def tile_copy(o):
        oz, oy = offsets(o // X)
        to_snap = ((z + oz) % Z) * Y + (y + oy) % Y
        to_x = (x + o % X) % X
        to = to_snap * X + to_x
        return pltpu.make_async_remote_copy(
            src_ref=send.at[to],
            dst_ref=recv.at[snap, x],
            send_sem=b_send.at[to],
            recv_sem=b_recv.at[snap],
            device_id=dev(to_snap, to_x, zc),
            device_id_type=MESH,
        )

    @pl.loop(1, D)
    def _(o):
        tile_copy(o).start()

    recv[snap, x] = send[me]
    inputs[3].wait()
    inputs[4].wait()

    lane = lax.broadcasted_iota(jnp.int32, (1, 2 * HALF), 1)
    turn = jnp.where(lane < HALF, 0.0, 0.25).astype(F32)
    for d in range(D):
        seg = uv[:, d * HALF : (d + 1) * HALF].astype(F32)
        uvs[d] = jnp.concatenate([seg, seg], axis=1)
    unp[...] = jnp.zeros_like(unp)
    acc[...] = jnp.zeros_like(acc)

    def phasor_rows(i):
        at = pl.multiple_of(i * 128, 128)
        far = pl.multiple_of(x * (OWN * BLOCK_PIX) + i * 128, 128)
        left = jnp.broadcast_to(lm[0:1, pl.ds(far, 128)], (128, 128)).T
        right = jnp.broadcast_to(lm[1:2, pl.ds(far, 128)], (128, 128)).T
        for d in range(D):
            turns = left * uvs[d, 0:1] + right * uvs[d, 1:2] + turn
            rest = turns - jnp.round(turns)
            t = rest * rest
            value = jnp.full_like(t, COS[-1])
            for coefficient in COS[-2::-1]:
                value = value * t + coefficient
            ph[pl.ds(at, 128), d * 128 : (d + 1) * 128] = value.astype(BF16)

    parts = OWN * BLOCK_PIX // 128 // S

    @pl.loop(0, S)
    def _(g):
        @pl.loop(0, parts)
        def _(i):
            phasor_rows(g * parts + i)

        src = source(g)
        fetch(src).wait()

        @pl.when(g == 0)
        def _():
            part = recv.at[snap, pl.ds(0, X - 1)]
            pltpu.make_async_copy(part, part, b_recv.at[snap]).wait()

        @pl.when(g > 0)
        def _():
            pltpu.make_async_copy(recv.at[src], recv.at[src], b_recv.at[src]).wait()

        for xs in range(X):
            for q in range(2):
                unp[xs * 2 + q, 0 : CH * 16] = (
                    recv[src, xs, q].reshape(CH * 16, TILE_PIX).astype(F32)
                )
        for b in range(OWN):
            lhs = jnp.concatenate(
                [
                    jnp.concatenate(
                        [unp[xs * 2 + q, pl.ds(j * 4 + b, 8, stride=16)] for xs in range(X)], axis=0
                    ).astype(BF16)
                    for q in range(2)
                    for j in range(4)
                ],
                axis=1,
            )
            weights = kbuf[src, :, b].reshape(SN * TILE_PIX, BLOCK_PIX)
            acc[b] += jnp.dot(lhs, weights, preferred_element_type=F32)

    def sum_copy(o):
        to = (me + o) % D
        return pltpu.make_async_remote_copy(
            src_ref=ubuf.at[to],
            dst_ref=g1.at[me],
            send_sem=g1_send.at[o],
            recv_sem=g1_recv.at[0],
            device_id=dev(to // X, to % X, zc),
            device_id_type=MESH,
        )

    cube = jnp.concatenate([acc[b].astype(BF16) for b in range(OWN)], axis=1)
    for n in range(0, D, X):
        part = jnp.dot(
            cube, ph[:, n * 128 : (n + X) * 128], preferred_element_type=F32
        ).astype(BF16)
        for i in range(X):
            ubuf[n + i] = part[:, i * 128 : (i + 1) * 128]

    @pl.loop(1, D)
    def _(o):
        sum_copy(o).start()

    g1[me] = ubuf[me]

    def cube_copy(o):
        to = (x + o) % X
        return pltpu.make_async_remote_copy(
            src_ref=acc.at[:, pl.ds(pl.multiple_of(to * 8, 8), 8), :],
            dst_ref=cubes.at[x],
            send_sem=d_send.at[o],
            recv_sem=d_recv.at[0],
            device_id=dev(snap, to, zc),
            device_id_type=MESH,
        )

    @pl.loop(1, X)
    def _(o):
        cube_copy(o).start()

    cubes[x] = acc[:, pl.ds(pl.multiple_of(x * 8, 8), 8), :]

    all_but_one = g1.at[pl.ds(0, D - 1)]
    pltpu.make_async_copy(all_but_one, all_but_one, g1_recv.at[0]).wait()
    total = g1[0].astype(F32)
    for d in range(1, D):
        total = total + g1[d].astype(F32)
    total = total.T.astype(BF16)
    each = HALF // G
    for to in range(G):
        g2_out[to] = jnp.concatenate(
            [total[r * HALF + to * each : r * HALF + (to + 1) * each] for r in range(2)], axis=0
        )

    def mode_copy(o):
        to = (zc + o) % G
        return pltpu.make_async_remote_copy(
            src_ref=g2_out.at[to],
            dst_ref=g2.at[zc],
            send_sem=g2_send.at[o],
            recv_sem=g2_recv.at[0],
            device_id=dev(snap, x, to),
            device_id_type=MESH,
        )

    @pl.loop(1, G)
    def _(o):
        mode_copy(o).start()

    g2[zc] = g2_out[zc]

    three = cubes.at[pl.ds(0, X - 1)]
    pltpu.make_async_copy(three, three, d_recv.at[0]).wait()
    for xs in range(X):
        for b in range(OWN):
            sky[:, xs * OWN + b, :] = cubes[xs, b, 0:CH]
    inputs[5].wait()

    all_but_one = g2.at[pl.ds(0, G - 1)]
    pltpu.make_async_copy(all_but_one, all_but_one, g2_recv.at[0]).wait()
    modes = jnp.concatenate([g2[i] for i in range(G)], axis=1)
    whole = jnp.dot(modes, mats[0], preferred_element_type=F32)
    whole += jnp.dot(modes, mats[1], preferred_element_type=F32)
    chans = X * G * CH
    delay[0] = whole[:each, :chans] + whole[each:, SIN : SIN + chans]
    delay[1] = whole[each:, :chans] - whole[:each, SIN : SIN + chans]

    @pl.loop(1, D)
    def _(o):
        tile_copy(o).wait_send()

    @pl.loop(1, X)
    def _(o):
        cube_copy(o).wait_send()

    @pl.loop(1, D)
    def _(o):
        sum_copy(o).wait_send()

    @pl.loop(1, G)
    def _(o):
        mode_copy(o).wait_send()


def per_device(snap_tiles, beam_gain, kernel, tile_map, pixel_lm, mode_uv):
    S = lax.axis_size("snap")
    G = lax.axis_size("chan") // X
    pixels = pixel_lm.shape[1]
    mats = jnp.asarray(delay_matrices(G, pixels * S))
    chans = G * X * CH
    vmem = pl.BlockSpec(memory_space=pltpu.VMEM)
    dma = pltpu.SemaphoreType.DMA
    cube, spec = pl.pallas_call(
        functools.partial(kernel_body, S, G),
        out_shape=(
            jax.ShapeDtypeStruct((CH, X * OWN, BLOCK_PIX), F32),
            jax.ShapeDtypeStruct((2, HALF // G, chans), F32),
        ),
        in_specs=[pl.BlockSpec(memory_space=pltpu.HBM)] * 7,
        out_specs=(vmem, vmem),
        scratch_shapes=[
            *(
                pltpu.VMEM(a.shape, a.dtype)
                for a in (snap_tiles, beam_gain, tile_map, pixel_lm, mode_uv, mats)
            ),
            dma((6,)),
            pltpu.VMEM((S, SN, OWN, TILE_PIX, BLOCK_PIX), BF16),
            pltpu.VMEM((OWN * BLOCK_PIX, S * X * 2 * HALF), BF16),
            pltpu.VMEM((S * X, 2, CH, 16, TILE_PIX), BF16),
            pltpu.VMEM((S, X, 2, CH, 16, TILE_PIX), BF16),
            pltpu.VMEM((X * 2, 128, TILE_PIX), F32),
            pltpu.VMEM((OWN, ROWS, BLOCK_PIX), F32),
            pltpu.VMEM((S * X, 2, 2 * HALF), F32),
            pltpu.VMEM((X, OWN, 8, BLOCK_PIX), F32),
            pltpu.VMEM((S * X, ROWS, 2 * HALF), BF16),
            pltpu.VMEM((S * X, ROWS, 2 * HALF), BF16),
            pltpu.VMEM((G, 2 * HALF // G, ROWS), BF16),
            pltpu.VMEM((G, 2 * HALF // G, ROWS), BF16),
            dma((S,)),
            dma((S * X,)),
            dma((S,)),
            dma((X,)),
            dma((1,)),
            dma((S * X,)),
            dma((1,)),
            dma((G,)),
            dma((1,)),
        ],
        compiler_params=pltpu.CompilerParams(
            collective_id=0, has_side_effects=True, vmem_limit_bytes=60 * 1024 * 1024
        ),
    )(snap_tiles, beam_gain, kernel, tile_map, pixel_lm, mode_uv, mats)
    return cube.transpose(1, 0, 2), spec.transpose(0, 2, 1)


def solution(mesh):
    return jax.shard_map(
        per_device,
        mesh=mesh,
        in_specs=(
            P("snap", "chan", None, None),
            P("snap", None, None),
            P(None, "snap", None, None),
            P(),
            P(None, "snap"),
            P(),
        ),
        out_specs=(P("snap", "chan", None), P(None, None, ("snap", "chan"))),
        check_vma=False,
    )
```

```python
import functools
import math

import jax
import jax.numpy as jnp
import ml_dtypes
import numpy as np
from jax import lax
from jax.experimental import pallas as pl
from jax.experimental.pallas import tpu as pltpu
from jax.sharding import PartitionSpec as P

MESH = pl.DeviceIdType.MESH
X = 4
Z = 2
TILES = 64
TILE_PIX = 128
BLOCK_PIX = 256
OWN = 4
SN = 8
CH = 6
ROWS = X * 8
HALF = 64
SIN = 256
F32 = jnp.float32
BF16 = jnp.bfloat16


def cosine_coefficients():
    fit = np.polynomial.chebyshev.Chebyshev.interpolate(
        lambda t: np.cos(2 * np.pi * np.sqrt(np.maximum(t, 0))), 5, domain=[0, 0.25]
    )
    return [float(c) for c in fit.convert(kind=np.polynomial.Polynomial).coef]


COS = cosine_coefficients()


def delay_matrices(groups, pixels):
    chans = groups * X * CH
    chan = np.arange(chans)
    window = 0.54 - 0.46 * np.cos(chan * (2 * math.pi / (chans - 1)))
    phase = (chan[:, None] * chan[None, :] % chans) * (2 * math.pi / chans)
    scale = window / math.sqrt(chans) / math.sqrt(pixels)
    out = np.zeros((groups * ROWS, 2 * SIN), np.float32)
    for zc in range(groups):
        for xr in range(X):
            row = zc * ROWS + xr * 8
            first = (xr * groups + zc) * CH
            part = slice(first, first + CH)
            out[row : row + CH, :chans] = np.cos(phase[part]) * scale[part, None]
            out[row : row + CH, SIN : SIN + chans] = np.sin(phase[part]) * scale[part, None]
    high = out.astype(ml_dtypes.bfloat16)
    low = (out - high.astype(np.float32)).astype(ml_dtypes.bfloat16)
    return np.stack([high, low])


def kernel_body(
    S, G, tiles_hbm, beam_hbm, kern, tmap_hbm, lm_hbm, uv_hbm, mats_hbm, sky, delay,
    tiles, beam, tmap, lm, uv, mats, in_sem, cube_low, sky_near, delay_near, out_sem, kbuf, ph, send, recv, unp, acc, uvs, cubes, ubuf, g1, g2_out, g2,
    k_sem, b_send, b_recv, d_send, d_recv, g1_send, g1_recv, g2_send, g2_recv,
):
    Y = S // Z
    D = S * X
    snap = lax.axis_index("snap")
    chan = lax.axis_index("chan")
    x, zc = chan // G, chan % G
    z, y = snap // Y, snap % Y
    me = snap * X + x

    def dev(to_snap, to_x, to_zc):
        return {"snap": to_snap, "chan": to_x * G + to_zc}

    def offsets(g):
        oz = g % 2
        return oz, (g // 2 + 2 * oz) % Y

    def source(g):
        oz, oy = offsets(g)
        return ((z + oz) % Z) * Y + (y + Y - oy) % Y

    def fetch(src):
        return pltpu.make_async_copy(
            kern.at[pl.ds(src * SN, SN), pl.ds(x * OWN, OWN)], kbuf.at[src], k_sem.at[src]
        )

    inputs = [
        pltpu.make_async_copy(far, near, in_sem.at[i])
        for i, (far, near) in enumerate(
            [
                (tmap_hbm, tmap), (tiles_hbm, tiles), (beam_hbm, beam),
                (uv_hbm, uv), (lm_hbm, lm), (mats_hbm, mats),
            ]
        )
    ]
    for copy in inputs:
        copy.start()

    barrier = pltpu.get_barrier_semaphore()

    @pl.loop(1, D)
    def _(o):
        other = (me + o) % D
        pl.semaphore_signal(
            barrier, inc=1, device_id=dev(other // X, other % X, zc), device_id_type=MESH
        )

    @pl.loop(1, G)
    def _(o):
        pl.semaphore_signal(
            barrier, inc=1, device_id=dev(snap, x, (zc + o) % G), device_id_type=MESH
        )

    @pl.loop(0, S)
    def _(g):
        fetch(source(g)).start()

    rows = D * 16
    blocks = D * OWN
    r_row = lax.broadcasted_iota(jnp.int32, (rows, blocks), 0)
    r_col = lax.broadcasted_iota(jnp.int32, (rows, blocks), 1)
    spread = jnp.where(r_col == (r_row // 16) * OWN + r_row % OWN, 1.0, 0.0).astype(BF16)
    k_row = lax.broadcasted_iota(jnp.int32, (rows, 4 * TILES), 0)
    k_col = lax.broadcasted_iota(jnp.int32, (rows, 4 * TILES), 1)
    same = (k_row // 4) % 4 == k_col // TILES
    wanted = jnp.where(same, k_col % TILES, -1).astype(F32)
    inputs[0].wait()
    own_map = tmap[pl.ds(pl.multiple_of(snap * SN, SN), SN), :].astype(F32)
    for q in range(2):
        wide = jnp.concatenate(
            [jnp.broadcast_to(own_map[q * 4 + j : q * 4 + j + 1], (TILES, blocks)) for j in range(4)],
            axis=0,
        ).astype(BF16)
        found = lax.dot_general(
            spread, wide, (((1,), (1,)), ((), ())), preferred_element_type=F32
        )
        if q == 0:
            inputs[1].wait()
            inputs[2].wait()
        onehot = jnp.where(found == wanted, 1.0, 0.0).astype(BF16)
        gain = beam[q * 4 : q * 4 + 4].reshape(4 * TILES, TILE_PIX)
        for c in range(0, CH, 2):
            pair = [
                (
                    tiles[q * 4 : q * 4 + 4, c + i].reshape(4 * TILES, TILE_PIX).astype(F32) * gain
                ).astype(BF16)
                for i in range(2)
            ]
            taken = jnp.dot(
                onehot, jnp.concatenate(pair, axis=1), preferred_element_type=F32
            ).astype(BF16)
            for i in range(2):
                send[:, q, c + i] = taken[:, i * TILE_PIX : (i + 1) * TILE_PIX].reshape(
                    D, 16, TILE_PIX
                )

    pl.semaphore_wait(barrier, D - 1 + G - 1)

    def tile_copy(o):
        oz, oy = offsets(o // X)
        to_snap = ((z + oz) % Z) * Y + (y + oy) % Y
        to_x = (x + o % X) % X
        to = to_snap * X + to_x
        return pltpu.make_async_remote_copy(
            src_ref=send.at[to],
            dst_ref=recv.at[snap, x],
            send_sem=b_send.at[to],
            recv_sem=b_recv.at[snap],
            device_id=dev(to_snap, to_x, zc),
            device_id_type=MESH,
        )

    @pl.loop(1, D)
    def _(o):
        tile_copy(o).start()

    recv[snap, x] = send[me]
    inputs[3].wait()
    inputs[4].wait()

    lane = lax.broadcasted_iota(jnp.int32, (1, 2 * HALF), 1)
    turn = jnp.where(lane < HALF, 0.0, 0.25).astype(F32)
    for d in range(D):
        seg = uv[:, d * HALF : (d + 1) * HALF].astype(F32)
        uvs[d] = jnp.concatenate([seg, seg], axis=1)
    unp[...] = jnp.zeros_like(unp)
    acc[...] = jnp.zeros_like(acc)

    def phasor_rows(i):
        at = pl.multiple_of(i * 128, 128)
        far = pl.multiple_of(x * (OWN * BLOCK_PIX) + i * 128, 128)
        left = jnp.broadcast_to(lm[0:1, pl.ds(far, 128)], (128, 128)).T
        right = jnp.broadcast_to(lm[1:2, pl.ds(far, 128)], (128, 128)).T
        for d in range(D):
            turns = left * uvs[d, 0:1] + right * uvs[d, 1:2] + turn
            rest = turns - jnp.round(turns)
            t = rest * rest
            value = jnp.full_like(t, COS[-1])
            for coefficient in COS[-2::-1]:
                value = value * t + coefficient
            ph[pl.ds(at, 128), d * 128 : (d + 1) * 128] = value.astype(BF16)

    parts = OWN * BLOCK_PIX // 128 // S

    @pl.loop(0, S)
    def _(g):
        @pl.loop(0, parts)
        def _(i):
            phasor_rows(g * parts + i)

        src = source(g)
        fetch(src).wait()

        @pl.when(g == 0)
        def _():
            part = recv.at[snap, pl.ds(0, X - 1)]
            pltpu.make_async_copy(part, part, b_recv.at[snap]).wait()

        @pl.when(g > 0)
        def _():
            pltpu.make_async_copy(recv.at[src], recv.at[src], b_recv.at[src]).wait()

        for xs in range(X):
            for q in range(2):
                unp[xs * 2 + q, 0 : CH * 16] = (
                    recv[src, xs, q].reshape(CH * 16, TILE_PIX).astype(F32)
                )
        for b in range(OWN):
            lhs = jnp.concatenate(
                [
                    jnp.concatenate(
                        [unp[xs * 2 + q, pl.ds(j * 4 + b, 8, stride=16)] for xs in range(X)], axis=0
                    ).astype(BF16)
                    for q in range(2)
                    for j in range(4)
                ],
                axis=1,
            )
            weights = kbuf[src, :, b].reshape(SN * TILE_PIX, BLOCK_PIX)
            acc[b] += jnp.dot(lhs, weights, preferred_element_type=F32)

    def sum_copy(to_snap, to_x):
        to = to_snap * X + to_x
        return pltpu.make_async_remote_copy(
            src_ref=ubuf.at[to],
            dst_ref=g1.at[me],
            send_sem=g1_send.at[to],
            recv_sem=g1_recv.at[0],
            device_id=dev(to_snap, to_x, zc),
            device_id_type=MESH,
        )

    cube_low[...] = jnp.concatenate([acc[b].astype(BF16) for b in range(OWN)], axis=1)

    @pl.loop(1, S + 1)
    def _(o):
        to_snap = (snap + o) % S
        at = pl.multiple_of(to_snap * (X * 128), X * 128)
        part = jnp.dot(
            cube_low[...], ph[:, pl.ds(at, X * 128)], preferred_element_type=F32
        ).astype(BF16)
        for i in range(X):
            ubuf[to_snap * X + i] = part[:, i * 128 : (i + 1) * 128]

        @pl.when(o < S)
        def _():
            sum_copy(to_snap, x).start()

        @pl.loop(1, X)
        def _(i):
            sum_copy(to_snap, (x + i) % X).start()

    g1[me] = ubuf[me]

    def cube_copy(o):
        to = (x + o) % X
        return pltpu.make_async_remote_copy(
            src_ref=acc.at[:, pl.ds(pl.multiple_of(to * 8, 8), 8), :],
            dst_ref=cubes.at[x],
            send_sem=d_send.at[o],
            recv_sem=d_recv.at[0],
            device_id=dev(snap, to, zc),
            device_id_type=MESH,
        )

    @pl.loop(1, X)
    def _(o):
        cube_copy(o).start()

    cubes[x] = acc[:, pl.ds(pl.multiple_of(x * 8, 8), 8), :]

    all_but_one = g1.at[pl.ds(0, D - 1)]
    pltpu.make_async_copy(all_but_one, all_but_one, g1_recv.at[0]).wait()
    total = g1[0].astype(F32)
    for d in range(1, D):
        total = total + g1[d].astype(F32)
    total = total.T
    each = HALF // G
    for to in range(G):
        g2_out[to] = jnp.concatenate(
            [total[r * HALF + to * each : r * HALF + (to + 1) * each] for r in range(2)], axis=0
        ).astype(BF16)

    def mode_copy(o):
        to = (zc + o) % G
        return pltpu.make_async_remote_copy(
            src_ref=g2_out.at[to],
            dst_ref=g2.at[zc],
            send_sem=g2_send.at[o],
            recv_sem=g2_recv.at[0],
            device_id=dev(snap, x, to),
            device_id_type=MESH,
        )

    @pl.loop(1, G)
    def _(o):
        mode_copy(o).start()

    g2[zc] = g2_out[zc]

    three = cubes.at[pl.ds(0, X - 1)]
    pltpu.make_async_copy(three, three, d_recv.at[0]).wait()
    for xs in range(X):
        for b in range(OWN):
            sky_near[:, xs * OWN + b, :] = cubes[xs, b, 0:CH]
    sky_copy = pltpu.make_async_copy(sky_near, sky, out_sem.at[0])
    sky_copy.start()
    inputs[5].wait()

    all_but_one = g2.at[pl.ds(0, G - 1)]
    pltpu.make_async_copy(all_but_one, all_but_one, g2_recv.at[0]).wait()
    modes = jnp.concatenate([g2[i] for i in range(G)], axis=1)
    whole = jnp.dot(modes, mats[0], preferred_element_type=F32)
    whole += jnp.dot(modes, mats[1], preferred_element_type=F32)
    chans = X * G * CH
    delay_near[0] = whole[:each, :chans] + whole[each:, SIN : SIN + chans]
    delay_near[1] = whole[each:, :chans] - whole[:each, SIN : SIN + chans]

    delay_copy = pltpu.make_async_copy(delay_near, delay, out_sem.at[1])
    delay_copy.start()

    @pl.loop(1, D)
    def _(o):
        tile_copy(o).wait_send()

    @pl.loop(1, X)
    def _(o):
        cube_copy(o).wait_send()

    @pl.loop(1, D)
    def _(o):
        to = (me + o) % D
        sum_copy(to // X, to % X).wait_send()

    @pl.loop(1, G)
    def _(o):
        mode_copy(o).wait_send()

    sky_copy.wait()
    delay_copy.wait()


def place(cube, spec, cube_out, spec_out, sem):
    copies = [
        pltpu.make_async_copy(cube, cube_out, sem.at[0]),
        pltpu.make_async_copy(spec, spec_out, sem.at[1]),
    ]
    for copy in copies:
        copy.start()
    for copy in copies:
        copy.wait()


def per_device(snap_tiles, beam_gain, kernel, tile_map, pixel_lm, mode_uv):
    S = lax.axis_size("snap")
    G = lax.axis_size("chan") // X
    pixels = pixel_lm.shape[1]
    mats = jnp.asarray(delay_matrices(G, pixels * S))
    chans = G * X * CH
    hbm = pl.BlockSpec(memory_space=pltpu.HBM)
    shapes = (
        jax.ShapeDtypeStruct((CH, X * OWN, BLOCK_PIX), F32),
        jax.ShapeDtypeStruct((2, HALF // G, chans), F32),
    )
    dma = pltpu.SemaphoreType.DMA
    cube, spec = pl.pallas_call(
        functools.partial(kernel_body, S, G),
        out_shape=shapes,
        in_specs=[hbm] * 7,
        out_specs=(hbm, hbm),
        scratch_shapes=[
            *(
                pltpu.VMEM(a.shape, a.dtype)
                for a in (snap_tiles, beam_gain, tile_map, pixel_lm, mode_uv, mats)
            ),
            dma((6,)),
            pltpu.VMEM((ROWS, OWN * BLOCK_PIX), BF16),
            pltpu.VMEM((CH, X * OWN, BLOCK_PIX), F32),
            pltpu.VMEM((2, HALF // G, chans), F32),
            dma((2,)),
            pltpu.VMEM((S, SN, OWN, TILE_PIX, BLOCK_PIX), BF16),
            pltpu.VMEM((OWN * BLOCK_PIX, S * X * 2 * HALF), BF16),
            pltpu.VMEM((S * X, 2, CH, 16, TILE_PIX), BF16),
            pltpu.VMEM((S, X, 2, CH, 16, TILE_PIX), BF16),
            pltpu.VMEM((X * 2, 128, TILE_PIX), F32),
            pltpu.VMEM((OWN, ROWS, BLOCK_PIX), F32),
            pltpu.VMEM((S * X, 2, 2 * HALF), F32),
            pltpu.VMEM((X, OWN, 8, BLOCK_PIX), F32),
            pltpu.VMEM((S * X, ROWS, 2 * HALF), BF16),
            pltpu.VMEM((S * X, ROWS, 2 * HALF), BF16),
            pltpu.VMEM((G, 2 * HALF // G, ROWS), BF16),
            pltpu.VMEM((G, 2 * HALF // G, ROWS), BF16),
            dma((S,)),
            dma((S * X,)),
            dma((S,)),
            dma((X,)),
            dma((1,)),
            dma((S * X,)),
            dma((1,)),
            dma((G,)),
            dma((1,)),
        ],
        compiler_params=pltpu.CompilerParams(
            collective_id=0, has_side_effects=True, vmem_limit_bytes=60 * 1024 * 1024
        ),
    )(snap_tiles, beam_gain, kernel, tile_map, pixel_lm, mode_uv, mats)
    cube, spec = pl.pallas_call(
        place,
        out_shape=shapes,
        in_specs=[hbm] * 2,
        out_specs=(hbm, hbm),
        scratch_shapes=[dma((2,))],
    )(cube, spec)
    return cube.transpose(1, 0, 2), spec.transpose(0, 2, 1)


def solution(mesh):
    return jax.shard_map(
        per_device,
        mesh=mesh,
        in_specs=(
            P("snap", "chan", None, None),
            P("snap", None, None),
            P(None, "snap", None, None),
            P(),
            P(None, "snap"),
            P(),
        ),
        out_specs=(P("snap", "chan", None), P(None, None, ("snap", "chan"))),
        check_vma=False,
    )
```

```python
import functools
import math

import jax
import jax.numpy as jnp
import ml_dtypes
import numpy as np
from jax import lax
from jax.experimental import pallas as pl
from jax.experimental.pallas import tpu as pltpu
from jax.sharding import PartitionSpec as P

MESH = pl.DeviceIdType.MESH
X = 4
Z = 2
TILES = 64
TILE_PIX = 128
BLOCK_PIX = 256
OWN = 4
SN = 8
CH = 6
ROWS = X * 8
HALF = 64
SIN = 256
F32 = jnp.float32
BF16 = jnp.bfloat16


def cosine_coefficients():
    fit = np.polynomial.chebyshev.Chebyshev.interpolate(
        lambda t: np.cos(2 * np.pi * np.sqrt(np.maximum(t, 0))), 5, domain=[0, 0.25]
    )
    return [float(c) for c in fit.convert(kind=np.polynomial.Polynomial).coef]


COS = cosine_coefficients()


def delay_matrices(groups, pixels):
    chans = groups * X * CH
    chan = np.arange(chans)
    window = 0.54 - 0.46 * np.cos(chan * (2 * math.pi / (chans - 1)))
    phase = (chan[:, None] * chan[None, :] % chans) * (2 * math.pi / chans)
    scale = window / math.sqrt(chans) / math.sqrt(pixels)
    out = np.zeros((groups * ROWS, 2 * SIN), np.float32)
    for zc in range(groups):
        for xr in range(X):
            row = zc * ROWS + xr * 8
            first = (xr * groups + zc) * CH
            part = slice(first, first + CH)
            out[row : row + CH, :chans] = np.cos(phase[part]) * scale[part, None]
            out[row : row + CH, SIN : SIN + chans] = np.sin(phase[part]) * scale[part, None]
    high = out.astype(ml_dtypes.bfloat16)
    low = (out - high.astype(np.float32)).astype(ml_dtypes.bfloat16)
    return np.stack([high, low])


def kernel_body(
    S, G, tiles_hbm, beam_hbm, kern, tmap_hbm, lm_hbm, uv_hbm, mats_hbm, sky, delay,
    tiles, beam, tmap, lm, uv, mats, in_sem, cube_low, sky_near, delay_near, out_sem, kbuf, ph, send, recv, unp, acc, uvs, cubes, ubuf, g1, g2_out, g2,
    k_sem, b_send, b_recv, d_send, d_recv, g1_send, g1_recv, g2_send, g2_recv,
):
    Y = S // Z
    D = S * X
    snap = lax.axis_index("snap")
    chan = lax.axis_index("chan")
    x, zc = chan // G, chan % G
    z, y = snap // Y, snap % Y
    me = snap * X + x

    def dev(to_snap, to_x, to_zc):
        return {"snap": to_snap, "chan": to_x * G + to_zc}

    def offsets(g):
        oz = g % 2
        return oz, (g // 2 + 2 * oz) % Y

    def source(g):
        oz, oy = offsets(g)
        return ((z + oz) % Z) * Y + (y + Y - oy) % Y

    def fetch(src):
        return pltpu.make_async_copy(
            kern.at[pl.ds(src * SN, SN), pl.ds(x * OWN, OWN)], kbuf.at[src], k_sem.at[src]
        )

    inputs = [
        pltpu.make_async_copy(far, near, in_sem.at[i])
        for i, (far, near) in enumerate(
            [
                (tmap_hbm, tmap), (tiles_hbm, tiles), (beam_hbm, beam),
                (uv_hbm, uv), (lm_hbm, lm), (mats_hbm, mats),
            ]
        )
    ]
    for copy in inputs:
        copy.start()

    barrier = pltpu.get_barrier_semaphore()

    @pl.loop(1, D)
    def _(o):
        other = (me + o) % D
        pl.semaphore_signal(
            barrier, inc=1, device_id=dev(other // X, other % X, zc), device_id_type=MESH
        )

    @pl.loop(1, G)
    def _(o):
        pl.semaphore_signal(
            barrier, inc=1, device_id=dev(snap, x, (zc + o) % G), device_id_type=MESH
        )

    @pl.loop(0, S)
    def _(g):
        fetch(source(g)).start()

    rows = D * 16
    blocks = D * OWN
    r_row = lax.broadcasted_iota(jnp.int32, (rows, blocks), 0)
    r_col = lax.broadcasted_iota(jnp.int32, (rows, blocks), 1)
    spread = jnp.where(r_col == (r_row // 16) * OWN + r_row % OWN, 1.0, 0.0).astype(BF16)
    k_row = lax.broadcasted_iota(jnp.int32, (rows, 4 * TILES), 0)
    k_col = lax.broadcasted_iota(jnp.int32, (rows, 4 * TILES), 1)
    same = (k_row // 4) % 4 == k_col // TILES
    wanted = jnp.where(same, k_col % TILES, -1).astype(F32)
    inputs[0].wait()
    own_map = tmap[pl.ds(pl.multiple_of(snap * SN, SN), SN), :].astype(F32)
    for q in range(2):
        wide = jnp.concatenate(
            [jnp.broadcast_to(own_map[q * 4 + j : q * 4 + j + 1], (TILES, blocks)) for j in range(4)],
            axis=0,
        ).astype(BF16)
        found = lax.dot_general(
            spread, wide, (((1,), (1,)), ((), ())), preferred_element_type=F32
        )
        if q == 0:
            inputs[1].wait()
            inputs[2].wait()
        onehot = jnp.where(found == wanted, 1.0, 0.0).astype(BF16)
        gain = beam[q * 4 : q * 4 + 4].reshape(4 * TILES, TILE_PIX)
        for c in range(0, CH, 2):
            pair = [
                (
                    tiles[q * 4 : q * 4 + 4, c + i].reshape(4 * TILES, TILE_PIX).astype(F32) * gain
                ).astype(BF16)
                for i in range(2)
            ]
            taken = jnp.dot(
                onehot, jnp.concatenate(pair, axis=1), preferred_element_type=F32
            ).astype(BF16)
            for i in range(2):
                send[:, q, c + i] = taken[:, i * TILE_PIX : (i + 1) * TILE_PIX].reshape(
                    D, 16, TILE_PIX
                )

    pl.semaphore_wait(barrier, D - 1 + G - 1)

    def tile_copy(o):
        oz, oy = offsets(o // X)
        to_snap = ((z + oz) % Z) * Y + (y + oy) % Y
        to_x = (x + o % X) % X
        to = to_snap * X + to_x
        return pltpu.make_async_remote_copy(
            src_ref=send.at[to],
            dst_ref=recv.at[snap, x],
            send_sem=b_send.at[to],
            recv_sem=b_recv.at[snap],
            device_id=dev(to_snap, to_x, zc),
            device_id_type=MESH,
        )

    @pl.loop(1, D)
    def _(o):
        tile_copy(o).start()

    recv[snap, x] = send[me]
    inputs[3].wait()
    inputs[4].wait()

    lane = lax.broadcasted_iota(jnp.int32, (1, 2 * HALF), 1)
    turn = jnp.where(lane < HALF, 0.0, 0.25).astype(F32)
    for d in range(D):
        seg = uv[:, d * HALF : (d + 1) * HALF].astype(F32)
        uvs[d] = jnp.concatenate([seg, seg], axis=1)
    unp[...] = jnp.zeros_like(unp)
    acc[...] = jnp.zeros_like(acc)

    def phasor_rows(i):
        at = pl.multiple_of(i * 128, 128)
        far = pl.multiple_of(x * (OWN * BLOCK_PIX) + i * 128, 128)
        left = jnp.broadcast_to(lm[0:1, pl.ds(far, 128)], (128, 128)).T
        right = jnp.broadcast_to(lm[1:2, pl.ds(far, 128)], (128, 128)).T
        for d in range(D):
            turns = left * uvs[d, 0:1] + right * uvs[d, 1:2] + turn
            rest = turns - jnp.round(turns)
            t = rest * rest
            value = jnp.full_like(t, COS[-1])
            for coefficient in COS[-2::-1]:
                value = value * t + coefficient
            ph[pl.ds(at, 128), d * 128 : (d + 1) * 128] = value.astype(BF16)

    @pl.loop(0, OWN * BLOCK_PIX // 128)
    def _(i):
        phasor_rows(i)

    @pl.loop(0, S)
    def _(g):
        src = source(g)
        fetch(src).wait()

        @pl.when(g == 0)
        def _():
            part = recv.at[snap, pl.ds(0, X - 1)]
            pltpu.make_async_copy(part, part, b_recv.at[snap]).wait()

        @pl.when(g > 0)
        def _():
            pltpu.make_async_copy(recv.at[src], recv.at[src], b_recv.at[src]).wait()

        for xs in range(X):
            for q in range(2):
                unp[xs * 2 + q, 0 : CH * 16] = (
                    recv[src, xs, q].reshape(CH * 16, TILE_PIX).astype(F32)
                )
        for b in range(OWN):
            lhs = jnp.concatenate(
                [
                    jnp.concatenate(
                        [unp[xs * 2 + q, pl.ds(j * 4 + b, 8, stride=16)] for xs in range(X)], axis=0
                    ).astype(BF16)
                    for q in range(2)
                    for j in range(4)
                ],
                axis=1,
            )
            weights = kbuf[src, :, b].reshape(SN * TILE_PIX, BLOCK_PIX)
            acc[b] += jnp.dot(lhs, weights, preferred_element_type=F32)

    def sum_copy(to_snap, to_x):
        to = to_snap * X + to_x
        return pltpu.make_async_remote_copy(
            src_ref=ubuf.at[to],
            dst_ref=g1.at[me],
            send_sem=g1_send.at[to],
            recv_sem=g1_recv.at[0],
            device_id=dev(to_snap, to_x, zc),
            device_id_type=MESH,
        )

    cube_low[...] = jnp.concatenate([acc[b].astype(BF16) for b in range(OWN)], axis=1)

    for n in range(S):
        part = jnp.dot(
            cube_low[...], ph[:, n * X * 128 : (n + 1) * X * 128], preferred_element_type=F32
        ).astype(BF16)
        for i in range(X):
            ubuf[n * X + i] = part[:, i * 128 : (i + 1) * 128]

        @pl.when(n != snap)
        def _():
            sum_copy(n, x).start()

        @pl.loop(1, X)
        def _(i):
            sum_copy(n, (x + i) % X).start()

    g1[me] = ubuf[me]

    def cube_copy(o):
        to = (x + o) % X
        return pltpu.make_async_remote_copy(
            src_ref=acc.at[:, pl.ds(pl.multiple_of(to * 8, 8), 8), :],
            dst_ref=cubes.at[x],
            send_sem=d_send.at[o],
            recv_sem=d_recv.at[0],
            device_id=dev(snap, to, zc),
            device_id_type=MESH,
        )

    @pl.loop(1, X)
    def _(o):
        cube_copy(o).start()

    cubes[x] = acc[:, pl.ds(pl.multiple_of(x * 8, 8), 8), :]

    all_but_one = g1.at[pl.ds(0, D - 1)]
    pltpu.make_async_copy(all_but_one, all_but_one, g1_recv.at[0]).wait()
    total = g1[0].astype(F32)
    for d in range(1, D):
        total = total + g1[d].astype(F32)
    total = total.T
    each = HALF // G
    for to in range(G):
        g2_out[to] = jnp.concatenate(
            [total[r * HALF + to * each : r * HALF + (to + 1) * each] for r in range(2)], axis=0
        ).astype(BF16)

    def mode_copy(o):
        to = (zc + o) % G
        return pltpu.make_async_remote_copy(
            src_ref=g2_out.at[to],
            dst_ref=g2.at[zc],
            send_sem=g2_send.at[o],
            recv_sem=g2_recv.at[0],
            device_id=dev(snap, x, to),
            device_id_type=MESH,
        )

    @pl.loop(1, G)
    def _(o):
        mode_copy(o).start()

    g2[zc] = g2_out[zc]

    three = cubes.at[pl.ds(0, X - 1)]
    pltpu.make_async_copy(three, three, d_recv.at[0]).wait()
    for xs in range(X):
        for b in range(OWN):
            sky_near[:, xs * OWN + b, :] = cubes[xs, b, 0:CH]
    sky_copy = pltpu.make_async_copy(sky_near, sky, out_sem.at[0])
    sky_copy.start()
    inputs[5].wait()

    all_but_one = g2.at[pl.ds(0, G - 1)]
    pltpu.make_async_copy(all_but_one, all_but_one, g2_recv.at[0]).wait()
    modes = jnp.concatenate([g2[i] for i in range(G)], axis=1)
    whole = jnp.dot(modes, mats[0], preferred_element_type=F32)
    whole += jnp.dot(modes, mats[1], preferred_element_type=F32)
    chans = X * G * CH
    delay_near[0] = whole[:each, :chans] + whole[each:, SIN : SIN + chans]
    delay_near[1] = whole[each:, :chans] - whole[:each, SIN : SIN + chans]

    delay_copy = pltpu.make_async_copy(delay_near, delay, out_sem.at[1])
    delay_copy.start()

    @pl.loop(1, D)
    def _(o):
        tile_copy(o).wait_send()

    @pl.loop(1, X)
    def _(o):
        cube_copy(o).wait_send()

    @pl.loop(1, D)
    def _(o):
        to = (me + o) % D
        sum_copy(to // X, to % X).wait_send()

    @pl.loop(1, G)
    def _(o):
        mode_copy(o).wait_send()

    sky_copy.wait()
    delay_copy.wait()


def per_device(snap_tiles, beam_gain, kernel, tile_map, pixel_lm, mode_uv):
    S = lax.axis_size("snap")
    G = lax.axis_size("chan") // X
    pixels = pixel_lm.shape[1]
    mats = jnp.asarray(delay_matrices(G, pixels * S))
    chans = G * X * CH
    hbm = pl.BlockSpec(memory_space=pltpu.HBM)
    shapes = (
        jax.ShapeDtypeStruct((CH, X * OWN, BLOCK_PIX), F32),
        jax.ShapeDtypeStruct((2, HALF // G, chans), F32),
    )
    dma = pltpu.SemaphoreType.DMA
    cube, spec = pl.pallas_call(
        functools.partial(kernel_body, S, G),
        out_shape=shapes,
        in_specs=[hbm] * 7,
        out_specs=(hbm, hbm),
        scratch_shapes=[
            *(
                pltpu.VMEM(a.shape, a.dtype)
                for a in (snap_tiles, beam_gain, tile_map, pixel_lm, mode_uv, mats)
            ),
            dma((6,)),
            pltpu.VMEM((ROWS, OWN * BLOCK_PIX), BF16),
            pltpu.VMEM((CH, X * OWN, BLOCK_PIX), F32),
            pltpu.VMEM((2, HALF // G, chans), F32),
            dma((2,)),
            pltpu.VMEM((S, SN, OWN, TILE_PIX, BLOCK_PIX), BF16),
            pltpu.VMEM((OWN * BLOCK_PIX, S * X * 2 * HALF), BF16),
            pltpu.VMEM((S * X, 2, CH, 16, TILE_PIX), BF16),
            pltpu.VMEM((S, X, 2, CH, 16, TILE_PIX), BF16),
            pltpu.VMEM((X * 2, 128, TILE_PIX), F32),
            pltpu.VMEM((OWN, ROWS, BLOCK_PIX), F32),
            pltpu.VMEM((S * X, 2, 2 * HALF), F32),
            pltpu.VMEM((X, OWN, 8, BLOCK_PIX), F32),
            pltpu.VMEM((S * X, ROWS, 2 * HALF), BF16),
            pltpu.VMEM((S * X, ROWS, 2 * HALF), BF16),
            pltpu.VMEM((G, 2 * HALF // G, ROWS), BF16),
            pltpu.VMEM((G, 2 * HALF // G, ROWS), BF16),
            dma((S,)),
            dma((S * X,)),
            dma((S,)),
            dma((X,)),
            dma((1,)),
            dma((S * X,)),
            dma((1,)),
            dma((G,)),
            dma((1,)),
        ],
        compiler_params=pltpu.CompilerParams(
            collective_id=0, has_side_effects=True, vmem_limit_bytes=int(53.92 * 1024 * 1024)
        ),
    )(snap_tiles, beam_gain, kernel, tile_map, pixel_lm, mode_uv, mats)
    return cube.transpose(1, 0, 2), spec.transpose(0, 2, 1)


def solution(mesh):
    return jax.shard_map(
        per_device,
        mesh=mesh,
        in_specs=(
            P("snap", "chan", None, None),
            P("snap", None, None),
            P(None, "snap", None, None),
            P(),
            P(None, "snap"),
            P(),
        ),
        out_specs=(P("snap", "chan", None), P(None, None, ("snap", "chan"))),
        check_vma=False,
    )
```

```python
import functools
import math

import jax
import jax.numpy as jnp
import ml_dtypes
import numpy as np
from jax import lax
from jax.experimental import pallas as pl
from jax.experimental.pallas import tpu as pltpu
from jax.sharding import PartitionSpec as P

MESH = pl.DeviceIdType.MESH
X = 4
Z = 2
TILES = 64
TILE_PIX = 128
BLOCK_PIX = 256
OWN = 4
SN = 8
CH = 6
ROWS = X * 8
HALF = 64
SIN = 256
F32 = jnp.float32
BF16 = jnp.bfloat16


def cosine_coefficients():
    fit = np.polynomial.chebyshev.Chebyshev.interpolate(
        lambda t: np.cos(2 * np.pi * np.sqrt(np.maximum(t, 0))), 5, domain=[0, 0.25]
    )
    return [float(c) for c in fit.convert(kind=np.polynomial.Polynomial).coef]


COS = cosine_coefficients()


def delay_matrices(groups, pixels):
    chans = groups * X * CH
    chan = np.arange(chans)
    window = 0.54 - 0.46 * np.cos(chan * (2 * math.pi / (chans - 1)))
    phase = (chan[:, None] * chan[None, :] % chans) * (2 * math.pi / chans)
    scale = window / math.sqrt(chans) / math.sqrt(pixels)
    out = np.zeros((groups * ROWS, 2 * SIN), np.float32)
    for zc in range(groups):
        for xr in range(X):
            row = zc * ROWS + xr * 8
            first = (xr * groups + zc) * CH
            part = slice(first, first + CH)
            out[row : row + CH, :chans] = np.cos(phase[part]) * scale[part, None]
            out[row : row + CH, SIN : SIN + chans] = np.sin(phase[part]) * scale[part, None]
    high = out.astype(ml_dtypes.bfloat16)
    low = (out - high.astype(np.float32)).astype(ml_dtypes.bfloat16)
    return np.stack([high, low])


def kernel_body(
    S, G, tiles_hbm, beam_hbm, kern, tmap_hbm, lm_hbm, uv_hbm, mats_hbm, sky, delay,
    tiles, beam, tmap, lm, uv, mats, in_sem, cube_low, sky_near, delay_near, out_sem, kbuf, ph, send, recv, unp, acc, uvs, cubes, ubuf, g1, g2_out, g2,
    k_sem, b_send, b_recv, d_send, d_recv, g1_send, g1_recv, g2_send, g2_recv,
):
    Y = S // Z
    D = S * X
    snap = lax.axis_index("snap")
    chan = lax.axis_index("chan")
    x, zc = chan // G, chan % G
    z, y = snap // Y, snap % Y
    me = snap * X + x

    def dev(to_snap, to_x, to_zc):
        return {"snap": to_snap, "chan": to_x * G + to_zc}

    def offsets(g):
        oz = g % 2
        return oz, (g // 2 + 2 * oz) % Y

    def source(g):
        oz, oy = offsets(g)
        return ((z + oz) % Z) * Y + (y + Y - oy) % Y

    def fetch(src):
        return pltpu.make_async_copy(
            kern.at[pl.ds(src * SN, SN), pl.ds(x * OWN, OWN)], kbuf.at[src], k_sem.at[src]
        )

    inputs = [
        pltpu.make_async_copy(far, near, in_sem.at[i])
        for i, (far, near) in enumerate(
            [
                (tmap_hbm, tmap), (tiles_hbm, tiles), (beam_hbm, beam),
                (uv_hbm, uv), (lm_hbm, lm), (mats_hbm, mats),
            ]
        )
    ]
    for copy in inputs:
        copy.start()

    barrier = pltpu.get_barrier_semaphore()

    @pl.loop(1, D)
    def _(o):
        other = (me + o) % D
        pl.semaphore_signal(
            barrier, inc=1, device_id=dev(other // X, other % X, zc), device_id_type=MESH
        )

    @pl.loop(1, G)
    def _(o):
        pl.semaphore_signal(
            barrier, inc=1, device_id=dev(snap, x, (zc + o) % G), device_id_type=MESH
        )

    @pl.loop(0, S)
    def _(g):
        fetch(source(g)).start()

    rows = D * 16
    blocks = D * OWN
    r_row = lax.broadcasted_iota(jnp.int32, (rows, blocks), 0)
    r_col = lax.broadcasted_iota(jnp.int32, (rows, blocks), 1)
    spread = jnp.where(r_col == (r_row // 16) * OWN + r_row % OWN, 1.0, 0.0).astype(BF16)
    k_row = lax.broadcasted_iota(jnp.int32, (rows, 4 * TILES), 0)
    k_col = lax.broadcasted_iota(jnp.int32, (rows, 4 * TILES), 1)
    same = (k_row // 4) % 4 == k_col // TILES
    wanted = jnp.where(same, k_col % TILES, -1).astype(F32)
    inputs[0].wait()
    own_map = tmap[pl.ds(pl.multiple_of(snap * SN, SN), SN), :].astype(F32)
    for q in range(2):
        wide = jnp.concatenate(
            [jnp.broadcast_to(own_map[q * 4 + j : q * 4 + j + 1], (TILES, blocks)) for j in range(4)],
            axis=0,
        ).astype(BF16)
        found = lax.dot_general(
            spread, wide, (((1,), (1,)), ((), ())), preferred_element_type=F32
        )
        if q == 0:
            inputs[1].wait()
            inputs[2].wait()
        onehot = jnp.where(found == wanted, 1.0, 0.0).astype(BF16)
        gain = beam[q * 4 : q * 4 + 4].reshape(4 * TILES, TILE_PIX)
        for c in range(0, CH, 2):
            pair = [
                (
                    tiles[q * 4 : q * 4 + 4, c + i].reshape(4 * TILES, TILE_PIX).astype(F32) * gain
                ).astype(BF16)
                for i in range(2)
            ]
            taken = jnp.dot(
                onehot, jnp.concatenate(pair, axis=1), preferred_element_type=F32
            ).astype(BF16)
            for i in range(2):
                send[:, q, c + i] = taken[:, i * TILE_PIX : (i + 1) * TILE_PIX].reshape(
                    D, 16, TILE_PIX
                )

    pl.semaphore_wait(barrier, D - 1 + G - 1)

    def tile_copy(o):
        oz, oy = offsets(o // 8 * 2 + o % 2)
        to_snap = ((z + oz) % Z) * Y + (y + oy) % Y
        to_x = (x + (o % 8 // 2 + 2 * (o % 2))) % X
        to = to_snap * X + to_x
        return pltpu.make_async_remote_copy(
            src_ref=send.at[to],
            dst_ref=recv.at[snap, x],
            send_sem=b_send.at[to],
            recv_sem=b_recv.at[snap],
            device_id=dev(to_snap, to_x, zc),
            device_id_type=MESH,
        )

    @pl.loop(1, D)
    def _(o):
        tile_copy(o).start()

    recv[snap, x] = send[me]
    inputs[3].wait()
    inputs[4].wait()

    lane = lax.broadcasted_iota(jnp.int32, (1, 2 * HALF), 1)
    turn = jnp.where(lane < HALF, 0.0, 0.25).astype(F32)
    for d in range(D):
        seg = uv[:, d * HALF : (d + 1) * HALF].astype(F32)
        uvs[d] = jnp.concatenate([seg, seg], axis=1)
    unp[...] = jnp.zeros_like(unp)
    acc[...] = jnp.zeros_like(acc)

    def phasor_rows(i):
        at = pl.multiple_of(i * 128, 128)
        far = pl.multiple_of(x * (OWN * BLOCK_PIX) + i * 128, 128)
        left = jnp.broadcast_to(lm[0:1, pl.ds(far, 128)], (128, 128)).T
        right = jnp.broadcast_to(lm[1:2, pl.ds(far, 128)], (128, 128)).T
        for d in range(D):
            turns = left * uvs[d, 0:1] + right * uvs[d, 1:2] + turn
            rest = turns - jnp.round(turns)
            t = rest * rest
            value = jnp.full_like(t, COS[-1])
            for coefficient in COS[-2::-1]:
                value = value * t + coefficient
            ph[pl.ds(at, 128), d * 128 : (d + 1) * 128] = value.astype(BF16)

    @pl.loop(0, OWN * BLOCK_PIX // 128)
    def _(i):
        phasor_rows(i)

    @pl.loop(0, S)
    def _(g):
        src = source(g)
        fetch(src).wait()

        @pl.when(g == 0)
        def _():
            part = recv.at[snap, pl.ds(0, X - 1)]
            pltpu.make_async_copy(part, part, b_recv.at[snap]).wait()

        @pl.when(g > 0)
        def _():
            pltpu.make_async_copy(recv.at[src], recv.at[src], b_recv.at[src]).wait()

        for xs in range(X):
            for q in range(2):
                unp[xs * 2 + q, 0 : CH * 16] = (
                    recv[src, xs, q].reshape(CH * 16, TILE_PIX).astype(F32)
                )
        for b in range(OWN):
            lhs = jnp.concatenate(
                [
                    jnp.concatenate(
                        [unp[xs * 2 + q, pl.ds(j * 4 + b, 8, stride=16)] for xs in range(X)], axis=0
                    ).astype(BF16)
                    for q in range(2)
                    for j in range(4)
                ],
                axis=1,
            )
            weights = kbuf[src, :, b].reshape(SN * TILE_PIX, BLOCK_PIX)
            acc[b] += jnp.dot(lhs, weights, preferred_element_type=F32)

    def sum_copy(to_snap, to_x):
        to = to_snap * X + to_x
        return pltpu.make_async_remote_copy(
            src_ref=ubuf.at[to],
            dst_ref=g1.at[me],
            send_sem=g1_send.at[to],
            recv_sem=g1_recv.at[0],
            device_id=dev(to_snap, to_x, zc),
            device_id_type=MESH,
        )

    cube_low[...] = jnp.concatenate([acc[b].astype(BF16) for b in range(OWN)], axis=1)

    for n in range(S):
        part = jnp.dot(
            cube_low[...], ph[:, n * X * 128 : (n + 1) * X * 128], preferred_element_type=F32
        ).astype(BF16)
        for i in range(X):
            ubuf[n * X + i] = part[:, i * 128 : (i + 1) * 128]

        @pl.when(n != snap)
        def _():
            sum_copy(n, x).start()

        @pl.loop(1, X)
        def _(i):
            sum_copy(n, (x + i) % X).start()

    g1[me] = ubuf[me]

    def cube_copy(o):
        to = (x + o) % X
        return pltpu.make_async_remote_copy(
            src_ref=acc.at[:, pl.ds(pl.multiple_of(to * 8, 8), 8), :],
            dst_ref=cubes.at[x],
            send_sem=d_send.at[o],
            recv_sem=d_recv.at[0],
            device_id=dev(snap, to, zc),
            device_id_type=MESH,
        )

    @pl.loop(1, X)
    def _(o):
        cube_copy(o).start()

    cubes[x] = acc[:, pl.ds(pl.multiple_of(x * 8, 8), 8), :]

    all_but_one = g1.at[pl.ds(0, D - 1)]
    pltpu.make_async_copy(all_but_one, all_but_one, g1_recv.at[0]).wait()
    total = g1[0].astype(F32)
    for d in range(1, D):
        total = total + g1[d].astype(F32)
    total = total.T
    each = HALF // G
    for to in range(G):
        g2_out[to] = jnp.concatenate(
            [total[r * HALF + to * each : r * HALF + (to + 1) * each] for r in range(2)], axis=0
        ).astype(BF16)

    def mode_copy(o):
        to = (zc + o) % G
        return pltpu.make_async_remote_copy(
            src_ref=g2_out.at[to],
            dst_ref=g2.at[zc],
            send_sem=g2_send.at[o],
            recv_sem=g2_recv.at[0],
            device_id=dev(snap, x, to),
            device_id_type=MESH,
        )

    @pl.loop(1, G)
    def _(o):
        mode_copy(o).start()

    g2[zc] = g2_out[zc]

    three = cubes.at[pl.ds(0, X - 1)]
    pltpu.make_async_copy(three, three, d_recv.at[0]).wait()
    for xs in range(X):
        for b in range(OWN):
            sky_near[:, xs * OWN + b, :] = cubes[xs, b, 0:CH]
    sky_copy = pltpu.make_async_copy(sky_near, sky, out_sem.at[0])
    sky_copy.start()
    @pl.loop(1, D)
    def _(o):
        tile_copy(o).wait_send()

    @pl.loop(1, X)
    def _(o):
        cube_copy(o).wait_send()

    @pl.loop(1, D)
    def _(o):
        to = (me + o) % D
        sum_copy(to // X, to % X).wait_send()

    inputs[5].wait()

    all_but_one = g2.at[pl.ds(0, G - 1)]
    pltpu.make_async_copy(all_but_one, all_but_one, g2_recv.at[0]).wait()
    modes = jnp.concatenate([g2[i] for i in range(G)], axis=1)
    whole = jnp.dot(modes, mats[0], preferred_element_type=F32)
    whole += jnp.dot(modes, mats[1], preferred_element_type=F32)
    chans = X * G * CH
    delay_near[0] = whole[:each, :chans] + whole[each:, SIN : SIN + chans]
    delay_near[1] = whole[each:, :chans] - whole[:each, SIN : SIN + chans]

    delay_copy = pltpu.make_async_copy(delay_near, delay, out_sem.at[1])
    delay_copy.start()

    @pl.loop(1, G)
    def _(o):
        mode_copy(o).wait_send()

    sky_copy.wait()
    delay_copy.wait()


def per_device(snap_tiles, beam_gain, kernel, tile_map, pixel_lm, mode_uv):
    S = lax.axis_size("snap")
    G = lax.axis_size("chan") // X
    pixels = pixel_lm.shape[1]
    mats = jnp.asarray(delay_matrices(G, pixels * S))
    chans = G * X * CH
    hbm = pl.BlockSpec(memory_space=pltpu.HBM)
    shapes = (
        jax.ShapeDtypeStruct((CH, X * OWN, BLOCK_PIX), F32),
        jax.ShapeDtypeStruct((2, HALF // G, chans), F32),
    )
    dma = pltpu.SemaphoreType.DMA
    cube, spec = pl.pallas_call(
        functools.partial(kernel_body, S, G),
        out_shape=shapes,
        in_specs=[hbm] * 7,
        out_specs=(hbm, hbm),
        scratch_shapes=[
            *(
                pltpu.VMEM(a.shape, a.dtype)
                for a in (snap_tiles, beam_gain, tile_map, pixel_lm, mode_uv, mats)
            ),
            dma((6,)),
            pltpu.VMEM((ROWS, OWN * BLOCK_PIX), BF16),
            pltpu.VMEM((CH, X * OWN, BLOCK_PIX), F32),
            pltpu.VMEM((2, HALF // G, chans), F32),
            dma((2,)),
            pltpu.VMEM((S, SN, OWN, TILE_PIX, BLOCK_PIX), BF16),
            pltpu.VMEM((OWN * BLOCK_PIX, S * X * 2 * HALF), BF16),
            pltpu.VMEM((S * X, 2, CH, 16, TILE_PIX), BF16),
            pltpu.VMEM((S, X, 2, CH, 16, TILE_PIX), BF16),
            pltpu.VMEM((X * 2, 128, TILE_PIX), F32),
            pltpu.VMEM((OWN, ROWS, BLOCK_PIX), F32),
            pltpu.VMEM((S * X, 2, 2 * HALF), F32),
            pltpu.VMEM((X, OWN, 8, BLOCK_PIX), F32),
            pltpu.VMEM((S * X, ROWS, 2 * HALF), BF16),
            pltpu.VMEM((S * X, ROWS, 2 * HALF), BF16),
            pltpu.VMEM((G, 2 * HALF // G, ROWS), BF16),
            pltpu.VMEM((G, 2 * HALF // G, ROWS), BF16),
            dma((S,)),
            dma((S * X,)),
            dma((S,)),
            dma((X,)),
            dma((1,)),
            dma((S * X,)),
            dma((1,)),
            dma((G,)),
            dma((1,)),
        ],
        compiler_params=pltpu.CompilerParams(
            collective_id=0, has_side_effects=True, vmem_limit_bytes=int(53.92 * 1024 * 1024)
        ),
    )(snap_tiles, beam_gain, kernel, tile_map, pixel_lm, mode_uv, mats)
    return cube.transpose(1, 0, 2), spec.transpose(0, 2, 1)


def solution(mesh):
    return jax.shard_map(
        per_device,
        mesh=mesh,
        in_specs=(
            P("snap", "chan", None, None),
            P("snap", None, None),
            P(None, "snap", None, None),
            P(),
            P(None, "snap"),
            P(),
        ),
        out_specs=(P("snap", "chan", None), P(None, None, ("snap", "chan"))),
        check_vma=False,
    )
```
